32 devices in a mesh: dp: 4 (over y, x), expert: 8 (over z, core).
Axes of the slice: x: 2, y: 2, z: 4, core: 2. Of those that a mesh axis runs over, the one named last changes fastest.
Arguments:
- tokens: bfloat16 [4096, 2048], P(('dp', 'expert')), may hold values from -6 to 6
- out_grad: bfloat16 [4096, 2048], P(('dp', 'expert')), may hold values from -6 to 6
- expert_ids: int32 [4096, 8], P(('dp', 'expert')), may hold values from 0 to 15, all different within a row
- route_probs: bfloat16 [4096, 8], P(('dp', 'expert')), may hold values from 0.019897461 to 0.5
- w_gate: bfloat16 [16, 2048, 768], P('expert'), may hold values from -0.125 to 0.125
- w_up: bfloat16 [16, 2048, 768], P('expert'), may hold values from -0.125 to 0.125
- w_down: bfloat16 [16, 2048, 768], P('expert'), may hold values from -0.21875 to 0.21875
- decay_mask: int32 [16, 3], P('expert'), may hold values from 0 to 1
Outputs:
- grad_tokens: bfloat16 [4096, 2048], P(('dp', 'expert'))
- grad_probs: bfloat16 [4096, 8], P(('dp', 'expert'))
- new_gate: bfloat16 [16, 2048, 768], P('expert', 'dp')
- new_up: bfloat16 [16, 2048, 768], P('expert', 'dp')
- new_down: bfloat16 [16, 2048, 768], P('expert', 'dp')
The draws below stay inside these ranges and needn't reach their ends.
All inputs are finite; a program needn't handle non-finite values.
Results may differ from the reference program's by a relative error of at most 0.015.
Values may be sent and summed in bfloat16 or wider, within the bound.
A program may use at most 192 MiB of HBM per device.

```python
import math
import jax
import jax.numpy as jnp
from jax import lax

D = 2048
H = 768
TOP = 8
TOK_DEV = 128
EXPERTS = 16
CAP = 64
TOKENS = 4096
N_DP = 4
N_EXPERT = 8


def with_ends(result, own_key, low, largest):
    longest = result.shape.index(max(result.shape))
    spots = []
    for shift in (0, 1):
        where = [jax.random.randint(jax.random.fold_in(own_key, axis), (), 0, length) for axis, length in enumerate(result.shape)]
        where[longest] = (where[longest] + shift) % result.shape[longest]
        spots.append(tuple(where))
    return result.at[spots[0]].set(low).at[spots[1]].set(largest)


def block_levels(own_key, shape, split, least, high):
    def one(dim, shards_of):
        steps = jax.random.uniform(jax.random.fold_in(jax.random.fold_in(own_key, 6), dim), (shards_of,), jnp.float32, least / len(split), high / len(split))
        return jnp.repeat(jnp.exp(steps), shape[dim] // shards_of).reshape((-1,) + (1,) * (len(shape) - dim - 1))

    gain = one(*split[0])
    for cut in split[1:]:
        gain = gain * one(*cut)
    return gain


def picks_of(rng, rows, number_of, top, lift):
    ranking = jax.random.permutation(jax.random.fold_in(rng, 1), number_of)
    pull = ranking
    for power in range(3):
        pull = pull * pull // number_of
    pull = pull * lift // number_of
    lots = jax.random.randint(jax.random.fold_in(rng, 2), (rows, number_of), 0, 4096) + pull
    holders = jax.random.permutation(jax.random.fold_in(rng, 3), rows)[jnp.arange(number_of) % rows]
    lots = jnp.where(jnp.arange(rows)[:, None] == holders[None, :], 1 << 14, lots)
    score = lots * number_of + jnp.arange(number_of)
    return lax.top_k(score.astype(jnp.int32), top)[1].astype(jnp.int32)


def bell_draw(rng, extent, scale, limit, cuts=(), kind=jnp.bfloat16):
    gain = block_levels(rng, extent, cuts, -0.22, 0.18) if cuts else 1.0
    values = jax.random.normal(rng, extent, jnp.float32) * scale * gain
    return jnp.minimum(jnp.maximum(values, -limit), limit).astype(kind)


def setup_inputs(seed: int = 0) -> dict:
    key_list = jax.random.split(jax.random.key(seed), 9)
    return {
        "tokens": bell_draw(key_list[0], (TOKENS, D), 1.0, 6.0, ((0, 32),)),
        "out_grad": bell_draw(key_list[1], (TOKENS, D), 1.0, 6.0, ((0, 32),)),
        "expert_ids": picks_of(key_list[2], TOKENS, EXPERTS, TOP, 4096),
        "route_probs": jnp.clip(jnp.exp(math.log(0.5) - 3.224016 * jax.random.uniform(key_list[3], (TOKENS, TOP), jnp.float32) ** block_levels(key_list[3], (TOKENS, TOP), ((0, 32),), -0.2, 0.2)), 0.019897461, 0.5).astype(jnp.bfloat16),
        "w_gate": bell_draw(key_list[4], (EXPERTS, D, H), D ** -0.5, 0.125, ((0, 8),)),
        "w_up": bell_draw(key_list[5], (EXPERTS, D, H), D ** -0.5, 0.125, ((0, 8),)),
        "w_down": bell_draw(key_list[6], (EXPERTS, D, H), H ** -0.5, 0.21875, ((0, 8),)),
        "decay_mask": with_ends(jax.random.randint(key_list[7], (EXPERTS, 3), 0, 2), jax.random.fold_in(key_list[7], 1), 0, 1).astype(jnp.int32),
    }


step_size = 0.004
shrink_rate = 0.1

def fill_table(slot_row, values, empty):
    table = jnp.full((EXPERTS * CAP + 1,), empty, jnp.int32)
    return table.at[slot_row].set(values)[:-1]

def take_rows(padded, index):
    return padded[index]

def reference(tokens, out_grad, expert_ids, route_probs, w_gate, w_up, w_down, decay_mask):
    devices = N_DP * N_EXPERT
    assigns = TOK_DEV * TOP
    ids = expert_ids.reshape(devices, assigns)
    onehot = (ids[:, :, None] == jnp.arange(EXPERTS, dtype=jnp.int32)[None, None, :]).astype(jnp.int32)
    before = jnp.cumsum(onehot, axis=1) - onehot
    position = lax.optimization_barrier(jnp.sum(before * onehot, axis=2)).astype(jnp.int32)
    slots = jnp.where(position < CAP, ids * CAP + position, EXPERTS * CAP).astype(jnp.int32)
    order = jnp.arange(assigns, dtype=jnp.int32)
    slot_token = jax.vmap(lambda s: fill_table(s, order // TOP, TOK_DEV))(slots)
    slot_assign = jax.vmap(lambda s: fill_table(s, order, assigns))(slots)
    slot_token = slot_token.reshape(devices, EXPERTS, CAP).transpose(1, 0, 2)
    slot_assign = slot_assign.reshape(devices, EXPERTS, CAP).transpose(1, 0, 2)
    zero_rows = jnp.zeros((devices, 1, D), jnp.bfloat16)
    tok_pad = jnp.concatenate([tokens.reshape(devices, TOK_DEV, D), zero_rows], axis=1)
    grad_pad = jnp.concatenate([out_grad.reshape(devices, TOK_DEV, D), zero_rows], axis=1)
    prob_pad = jnp.concatenate([route_probs.reshape(devices, assigns), jnp.zeros((devices, 1), jnp.bfloat16)], axis=1)

    def group_grad(left, right):
        left_g = left.reshape(N_DP, N_EXPERT * CAP, -1).astype(jnp.float32)
        right_g = right.reshape(N_DP, N_EXPERT * CAP, -1).astype(jnp.float32)
        partial_g = jnp.einsum('prd,prh->pdh', left_g, right_g).astype(jnp.bfloat16)
        partial_g = lax.optimization_barrier(partial_g)
        return lax.optimization_barrier(jnp.sum(partial_g.astype(jnp.float32), axis=0))

    def expert_step(carry, inputs):
        dx_acc, dp_acc = carry
        tok_e, asg_e, weight_g, weight_u, weight_d, mask_e = inputs
        x_rows = jax.vmap(take_rows)(tok_pad, tok_e).reshape(devices * CAP, D)
        dy_rows = jax.vmap(take_rows)(grad_pad, tok_e).reshape(devices * CAP, D)
        p_rows = jax.vmap(take_rows)(prob_pad, asg_e).reshape(devices * CAP)
        gate = jnp.dot(x_rows, weight_g, preferred_element_type=jnp.float32)
        upper = jnp.dot(x_rows, weight_u, preferred_element_type=jnp.float32)
        sig = jax.nn.sigmoid(gate)
        act = gate * sig
        hid = (act * upper).astype(jnp.bfloat16)
        outs = jnp.dot(hid, weight_d.T, preferred_element_type=jnp.float32).astype(jnp.bfloat16)
        dp_rows = lax.optimization_barrier(jnp.sum(dy_rows.astype(jnp.float32) * outs.astype(jnp.float32), axis=1)).astype(jnp.bfloat16)
        dout = (p_rows.astype(jnp.float32)[:, None] * dy_rows.astype(jnp.float32)).astype(jnp.bfloat16)
        dhid = jnp.dot(dout, weight_d, preferred_element_type=jnp.float32)
        dgate = (dhid * upper * sig * (1.0 + gate * (1.0 - sig))).astype(jnp.bfloat16)
        dup = (dhid * act).astype(jnp.bfloat16)
        dx_rows = (jnp.dot(dgate, weight_g.T, preferred_element_type=jnp.float32) + jnp.dot(dup, weight_u.T, preferred_element_type=jnp.float32)).astype(jnp.bfloat16)
        grad_g = group_grad(x_rows, dgate)
        grad_u = group_grad(x_rows, dup)
        grad_d = group_grad(dout, hid)
        mask_f = mask_e.astype(jnp.float32)

        def update(weight, grad_w, rate):
            weight_f = weight.astype(jnp.float32)
            return (weight_f - step_size * grad_w - shrink_rate * rate * weight_f).astype(jnp.bfloat16)
        new_g = update(weight_g, grad_g, mask_f[0])
        new_u = update(weight_u, grad_u, mask_f[1])
        new_d = update(weight_d, grad_d, mask_f[2])
        dx_acc = jax.vmap(lambda acc, idx, val: acc.at[idx].add(val))(dx_acc, tok_e, dx_rows.reshape(devices, CAP, D).astype(jnp.float32))
        dp_acc = jax.vmap(lambda acc, idx, val: acc.at[idx].set(val))(dp_acc, asg_e, dp_rows.reshape(devices, CAP))
        return ((dx_acc, dp_acc), (new_g, new_u, new_d))
    dx_init = jnp.zeros((devices, TOK_DEV + 1, D), jnp.float32)
    dp_init = jnp.zeros((devices, assigns + 1), jnp.bfloat16)
    carry, updated = lax.scan(expert_step, (dx_init, dp_init), (slot_token, slot_assign, w_gate, w_up, w_down, decay_mask))
    dx_acc, dp_acc = carry
    grad_tokens = dx_acc[:, :TOK_DEV, :].reshape(TOKENS, D).astype(jnp.bfloat16)
    grad_probs = dp_acc[:, :assigns].reshape(TOKENS, TOP)
    return (grad_tokens, grad_probs, updated[0], updated[1], updated[2])
```

```python
import jax
import jax.numpy as jnp
from jax import lax
from jax.sharding import PartitionSpec as P

step_size = 0.004
shrink_rate = 0.1
F32 = jnp.float32
BF16 = jnp.bfloat16


def mm(spec, a, b, out=F32):
    r = jnp.einsum(spec, a, b, preferred_element_type=F32)
    return r if out == F32 else r.astype(out)


def body(tokens, out_grad, expert_ids, route_probs, w_gate, w_up, w_down, decay_mask):
    n_owner = lax.axis_size("expert")
    n_group = lax.axis_size("dp")
    local_exp = w_gate.shape[0]
    width = tokens.shape[1]
    hidden = w_gate.shape[2]
    tok_rows = tokens.shape[0]
    topk = expert_ids.shape[1]
    n_experts = n_owner * local_exp
    capacity = tok_rows * topk // n_experts
    me_q = lax.axis_index("expert")
    me_p = lax.axis_index("dp")
    lo = me_p % 2
    hi = me_p // 2
    shard_rows = width // n_group

    meta = jnp.concatenate([expert_ids.astype(BF16), route_probs], axis=1)
    all_meta = lax.all_gather(meta, "expert", axis=0, tiled=True)
    x_all = lax.all_gather(tokens, "expert", axis=0, tiled=True)
    dy_all = lax.all_gather(out_grad, "expert", axis=0, tiled=True)

    meta_b = all_meta.reshape(n_owner, tok_rows, 2 * topk).astype(F32)
    ids_b = meta_b[..., :topk].astype(jnp.int32)
    probs_b = meta_b[..., topk:]
    mine = me_q * local_exp + jnp.arange(local_exp, dtype=jnp.int32)
    hit = ids_b[:, None, :, :] == mine[None, :, None, None]
    picked = jnp.any(hit, axis=3)
    p_tok = jnp.sum(jnp.where(hit, probs_b[:, None], 0.0), axis=3)
    earlier = (
        jnp.arange(tok_rows)[:, None] < jnp.arange(tok_rows)[None, :]
    ).astype(BF16)
    position = mm("bes,st->bet", picked.astype(BF16), earlier).astype(jnp.int32)
    spot = jnp.where(picked, position, capacity)
    disp_bool = spot[:, :, None, :] == jnp.arange(capacity)[None, None, :, None]
    disp = disp_bool.astype(BF16)
    p_slot = jnp.sum(jnp.where(disp_bool, p_tok[:, :, None, :], 0.0), axis=3)
    p_slot = p_slot.transpose(1, 0, 2).reshape(local_exp, n_owner * capacity)
    slots = n_owner * capacity

    x_b = x_all.reshape(n_owner, tok_rows, width)
    rows_x = mm("bect,btd->ebcd", disp, x_b, BF16).reshape(local_exp, slots, width)
    gate = mm("erd,edh->erh", rows_x, w_gate)
    upper = mm("erd,edh->erh", rows_x, w_up)
    sig = jax.nn.sigmoid(gate)
    act = gate * sig
    hid_f = act * upper
    hid_p = (hid_f * p_slot[..., None]).astype(BF16)
    dact = upper * sig * (1.0 + gate * (1.0 - sig))

    dy_b = dy_all.reshape(n_owner, tok_rows, width)
    rows_dy = mm("bect,btd->ebcd", disp, dy_b, BF16).reshape(local_exp, slots, width)

    def pick(rows, axis_bit, which):
        v = rows.reshape(slots, 2, 2, shard_rows)
        axis = 2 if axis_bit == 1 else 1
        return lax.dynamic_index_in_dim(v, which, axis, keepdims=False)

    def swap(v, bit):
        return lax.ppermute(v, "dp", [(i, i ^ bit) for i in range(n_group)])

    def reduce_rows(left, right, bit):
        first, second = (lo, hi) if bit == 1 else (hi, lo)
        out = mm("rad,rh->adh", pick(left, bit, 1 - first), right, BF16)
        got = swap(out, bit)
        keep = mm("rad,rh->adh", pick(left, bit, first), right, BF16)
        half = keep.astype(F32) + got.astype(F32)
        own = lax.dynamic_index_in_dim(half, second, 0, keepdims=False)
        away = lax.dynamic_index_in_dim(half, 1 - second, 0, keepdims=False).astype(BF16)
        return own + swap(away, 3 - bit).astype(F32)

    bits = [1 + (e % 2) for e in range(local_exp)]
    g_down = [reduce_rows(rows_dy[e], hid_p[e], bits[e]) for e in range(local_exp)]

    u = mm("erd,edh->erh", rows_dy, w_down)
    dprob_slot = jnp.sum(u * hid_f.astype(BF16).astype(F32), axis=2)
    dhid = u * p_slot[..., None]
    dgate = (dhid * dact).astype(BF16)
    dup = (dhid * act).astype(BF16)
    g_gate = [reduce_rows(rows_x[e], dgate[e], bits[e]) for e in range(local_exp)]
    g_up = [reduce_rows(rows_x[e], dup[e], bits[e]) for e in range(local_exp)]

    dx = (mm("erh,edh->erd", dgate, w_gate) + mm("erh,edh->erd", dup, w_up)).astype(BF16)
    part = mm(
        "bect,ebcd->btd", disp, dx.reshape(local_exp, n_owner, capacity, width), BF16
    ).reshape(n_owner * tok_rows, width)
    grad_tokens = lax.psum_scatter(part, "expert", scatter_dimension=0, tiled=True)

    dprob = dprob_slot.reshape(local_exp, n_owner, capacity).transpose(1, 0, 2)
    q_tok = jnp.sum(jnp.where(disp_bool, dprob[..., None], 0.0), axis=2)
    q_got = lax.all_to_all(q_tok.astype(BF16), "expert", split_axis=0, concat_axis=0, tiled=True)
    q_got = q_got.reshape(n_experts, tok_rows).astype(F32)
    sel = expert_ids[:, :, None] == jnp.arange(n_experts, dtype=jnp.int32)[None, None, :]
    grad_probs = jnp.sum(jnp.where(sel, q_got.T[:, None, :], 0.0), axis=2).astype(BF16)

    rates = decay_mask.astype(F32)

    def update(weight, grads, column):
        own = lax.dynamic_slice_in_dim(weight, me_p * shard_rows, shard_rows, 1).astype(F32)
        factor = rates[:, column][:, None, None]
        return (own - step_size * jnp.stack(grads) - shrink_rate * factor * own).astype(BF16)

    return (
        grad_tokens,
        grad_probs,
        update(w_gate, g_gate, 0),
        update(w_up, g_up, 1),
        update(w_down, g_down, 2),
    )


def solution(mesh):
    placed = (
        P(("dp", "expert"), None),
        P(("dp", "expert"), None),
        P(("dp", "expert"), None),
        P(("dp", "expert"), None),
        P("expert", None, None),
        P("expert", None, None),
        P("expert", None, None),
        P("expert", None),
    )
    return jax.shard_map(
        body,
        mesh=mesh,
        in_specs=placed,
        out_specs=(
            P(("dp", "expert"), None),
            P(("dp", "expert"), None),
            P("expert", "dp", None),
            P("expert", "dp", None),
            P("expert", "dp", None),
        ),
        check_vma=False,
    )
```

```python
import jax
import jax.numpy as jnp
from jax import lax
from jax.sharding import PartitionSpec as P

step_size = 0.004
shrink_rate = 0.1
F32 = jnp.float32
BF16 = jnp.bfloat16


def mm(spec, a, b, out=F32):
    r = jnp.einsum(spec, a, b, preferred_element_type=F32)
    return r if out == F32 else r.astype(out)


def body(tokens, out_grad, expert_ids, route_probs, w_gate, w_up, w_down, decay_mask):
    n_owner = lax.axis_size("expert")
    n_group = lax.axis_size("dp")
    local_exp = w_gate.shape[0]
    width = tokens.shape[1]
    tok_rows = tokens.shape[0]
    topk = expert_ids.shape[1]
    n_experts = n_owner * local_exp
    capacity = tok_rows * topk // n_experts
    me_q = lax.axis_index("expert")
    me_p = lax.axis_index("dp")
    shard_rows = width // n_group

    def near(j):
        return jnp.bitwise_xor(me_p, 3 - j)

    def reorder(v, axis):
        parts = [
            lax.dynamic_slice_in_dim(v, near(j) * shard_rows, shard_rows, axis)
            for j in range(n_group)
        ]
        return jnp.concatenate(parts, axis=axis)

    def cut(v, j):
        return v[:, j * shard_rows : (j + 1) * shard_rows]

    def gather(v):
        return lax.all_gather(v, "expert", axis=0, tiled=True)

    def hold(*vals):
        return lax.optimization_barrier(vals)

    experts = range(local_exp)
    meta = jnp.concatenate([expert_ids.astype(BF16), route_probs], axis=1)
    all_meta = gather(meta)
    x_all = gather(reorder(tokens, 1))
    dy_own = reorder(out_grad, 1)
    half = 2 * shard_rows
    dy_a = gather(dy_own[:, :half])
    dy_b = gather(dy_own[:, half:])
    wg = [reorder(w_gate[e], 0) for e in experts]
    wu = [reorder(w_up[e], 0) for e in experts]
    wd = [reorder(w_down[e], 0) for e in experts]

    meta_b = all_meta.reshape(n_owner, tok_rows, 2 * topk).astype(F32)
    ids_b = meta_b[..., :topk].astype(jnp.int32)
    probs_b = meta_b[..., topk:]
    mine = me_q * local_exp + jnp.arange(local_exp, dtype=jnp.int32)
    hit = ids_b[:, None, :, :] == mine[None, :, None, None]
    picked = jnp.any(hit, axis=3)
    p_tok = jnp.sum(jnp.where(hit, probs_b[:, None], 0.0), axis=3)
    earlier = (
        jnp.arange(tok_rows)[:, None] < jnp.arange(tok_rows)[None, :]
    ).astype(BF16)
    position = mm("bes,st->bet", picked.astype(BF16), earlier).astype(jnp.int32)
    spot = jnp.where(picked, position, capacity)
    slots = n_owner * capacity
    taken, disp, p_slot = [], [], []
    for e in experts:
        fits = spot[:, e, None, :] == jnp.arange(capacity)[None, :, None]
        taken.append(fits)
        disp.append(fits.astype(BF16))
        p_slot.append(
            jnp.sum(jnp.where(fits, p_tok[:, e, None, :], 0.0), axis=2).reshape(slots, 1)
        )

    def dispatch(e, rows_all):
        rows = rows_all.reshape(n_owner, tok_rows, rows_all.shape[1])
        return mm("bct,btd->bcd", disp[e], rows, BF16).reshape(slots, rows_all.shape[1])

    rows_x, act, dact, hid, hid_p = [], [], [], [], []
    for e in experts:
        rows_x.append(dispatch(e, x_all))
        gate = mm("rd,dh->rh", rows_x[e], wg[e])
        upper = mm("rd,dh->rh", rows_x[e], wu[e])
        sig = jax.nn.sigmoid(gate)
        act.append(gate * sig)
        dact.append(upper * sig * (1.0 + gate * (1.0 - sig)))
        hid.append(act[e] * upper)
        hid_p.append((hid[e] * p_slot[e]).astype(BF16))

    def swap(v, bit):
        return lax.ppermute(v, "dp", [(i, i ^ bit) for i in range(n_group)])

    def term(left, right):
        return mm("rd,rh->dh", left, right, BF16)

    bits = [1 + (e % 2) for e in experts]

    def finish(e, far, own_got, left_next, left_own, right):
        away = (term(left_next, right).astype(F32) + far.astype(F32)).astype(BF16)
        last = swap(away, 3 - bits[e])
        return term(left_own, right).astype(F32) + own_got.astype(F32) + last.astype(F32)

    flat = hold(dy_a, *hid_p)
    dy_a, hid_p = flat[0], list(flat[1:])
    rows_a = [dispatch(e, dy_a) for e in experts]
    down_far = [swap(term(cut(rows_a[e], 0), hid_p[e]), bits[e]) for e in experts]
    down_own = [
        swap(term(cut(rows_a[e], 1), hid_p[e]), 2) if bits[e] == 2 else None for e in experts
    ]
    flat = hold(dy_b, *down_far)
    dy_b, down_far = flat[0], list(flat[1:])
    rows_b = [dispatch(e, dy_b) for e in experts]
    sent = [term(cut(rows_b[e], 0), hid_p[e]) for e in experts if bits[e] == 1]
    flat = hold(*rows_b, *sent)
    rows_b, sent = list(flat[:local_exp]), list(flat[local_exp:])
    for e in experts:
        if bits[e] == 1:
            down_own[e] = swap(sent.pop(0), 1)

    dprob_slot, dgate, dup = [], [], []
    for e in experts:
        u = mm("rd,dh->rh", jnp.concatenate([rows_a[e], rows_b[e]], axis=1), wd[e])
        dprob_slot.append(jnp.sum(u * hid[e].astype(BF16).astype(F32), axis=1))
        dhid = u * p_slot[e]
        dgate.append((dhid * dact[e]).astype(BF16))
        dup.append((dhid * act[e]).astype(BF16))

    rights = [r for e in experts for r in (dgate[e], dup[e])]
    who = [e for e in experts for _ in range(2)]
    first_pos = [3 - bits[e] for e in experts]
    send_far = [term(cut(rows_x[e], 0), r) for e, r in zip(who, rights)]
    send_own = [term(cut(rows_x[e], first_pos[e]), r) for e, r in zip(who, rights)]
    n_far = len(send_far)
    flat = hold(*send_far, *send_own, *rights)
    send_far, send_own, late = flat[:n_far], flat[n_far : 2 * n_far], flat[2 * n_far :]
    got_far = [swap(v, bits[e]) for e, v in zip(who, send_far)]
    got_own = [swap(v, bits[e]) for e, v in zip(who, send_own)]

    late = list(late)
    flat = hold(*late, *got_far[0::2])
    late = flat[: len(late)]
    got_far[0::2] = flat[len(late) :]
    part = 0.0
    for e in experts:
        dx = mm("rh,dh->rd", late[2 * e], wg[e]) + mm("rh,dh->rd", late[2 * e + 1], wu[e])
        dx = dx.astype(BF16).reshape(n_owner, capacity, width)
        part = part + mm("bct,bcd->btd", disp[e], dx)
    part = part.astype(BF16).reshape(n_owner * tok_rows, width)
    flat = hold(part, *got_far[1::2], *got_own[0::2])
    part = flat[0]
    got_far[1::2] = flat[1 : 1 + local_exp]
    got_own[0::2] = flat[1 + local_exp :]
    summed = lax.psum_scatter(part, "expert", scatter_dimension=0, tiled=True)
    grad_tokens = jnp.concatenate(
        [
            lax.dynamic_slice_in_dim(
                summed, (3 - jnp.bitwise_xor(me_p, s)) * shard_rows, shard_rows, 1
            )
            for s in range(n_group)
        ],
        axis=1,
    )

    next_pos = [bits[e] for e in experts]
    own_pos = n_group - 1
    g_down = [
        finish(
            e,
            down_far[e],
            down_own[e],
            cut(rows_a[e], 1) if next_pos[e] == 1 else cut(rows_b[e], 0),
            cut(rows_b[e], 1),
            hid_p[e],
        )
        for e in experts
    ]
    g_rest = [
        finish(
            e, got_far[i], got_own[i], cut(rows_x[e], next_pos[e]), cut(rows_x[e], own_pos), r
        )
        for i, (e, r) in enumerate(zip(who, rights))
    ]
    g_gate, g_up = g_rest[0::2], g_rest[1::2]

    q_tok = jnp.stack(
        [
            jnp.sum(
                jnp.where(taken[e], dprob_slot[e].reshape(n_owner, capacity, 1), 0.0), axis=1
            )
            for e in experts
        ],
        axis=1,
    )
    q_got = lax.all_to_all(q_tok.astype(BF16), "expert", split_axis=0, concat_axis=0, tiled=True)
    q_got = q_got.reshape(n_experts, tok_rows).astype(F32)
    sel = expert_ids[:, :, None] == jnp.arange(n_experts, dtype=jnp.int32)[None, None, :]
    grad_probs = jnp.sum(jnp.where(sel, q_got.T[:, None, :], 0.0), axis=2).astype(BF16)

    rates = decay_mask.astype(F32)

    def update(weights, grads, column):
        out = []
        for e in experts:
            own = weights[e][own_pos * shard_rows :].astype(F32)
            out.append(
                own - step_size * grads[e] - shrink_rate * rates[e, column] * own
            )
        return jnp.stack(out).astype(BF16)

    return (
        grad_tokens,
        grad_probs,
        update(wg, g_gate, 0),
        update(wu, g_up, 1),
        update(wd, g_down, 2),
    )


def solution(mesh):
    placed = (
        P(("dp", "expert"), None),
        P(("dp", "expert"), None),
        P(("dp", "expert"), None),
        P(("dp", "expert"), None),
        P("expert", None, None),
        P("expert", None, None),
        P("expert", None, None),
        P("expert", None),
    )
    return jax.shard_map(
        body,
        mesh=mesh,
        in_specs=placed,
        out_specs=(
            P(("dp", "expert"), None),
            P(("dp", "expert"), None),
            P("expert", "dp", None),
            P("expert", "dp", None),
            P("expert", "dp", None),
        ),
        check_vma=False,
    )
```

```python
import jax
import jax.numpy as jnp
from jax import lax
from jax.sharding import PartitionSpec as P

step_size = 0.004
shrink_rate = 0.1
F32 = jnp.float32
BF16 = jnp.bfloat16


def mm(spec, a, b, out=F32):
    r = jnp.einsum(spec, a, b, preferred_element_type=F32)
    return r if out == F32 else r.astype(out)


def body(tokens, out_grad, expert_ids, route_probs, w_gate, w_up, w_down, decay_mask):
    n_owner = lax.axis_size("expert")
    n_group = lax.axis_size("dp")
    local_exp = w_gate.shape[0]
    width = tokens.shape[1]
    tok_rows = tokens.shape[0]
    topk = expert_ids.shape[1]
    n_experts = n_owner * local_exp
    capacity = tok_rows * topk // n_experts
    me_q = lax.axis_index("expert")
    me_p = lax.axis_index("dp")
    shard_rows = width // n_group

    def near(j):
        return jnp.bitwise_xor(me_p, 3 - j)

    def reorder(v, axis):
        parts = [
            lax.dynamic_slice_in_dim(v, near(j) * shard_rows, shard_rows, axis)
            for j in range(n_group)
        ]
        return jnp.concatenate(parts, axis=axis)

    def cut(v, j):
        return v[:, j * shard_rows : (j + 1) * shard_rows]

    def gather(v):
        return lax.all_gather(v, "expert", axis=0, tiled=True)

    def hold(*vals):
        return lax.optimization_barrier(vals)

    experts = range(local_exp)
    meta = jnp.concatenate([expert_ids.astype(BF16), route_probs], axis=1)
    all_meta = gather(meta)
    x_all = gather(reorder(tokens, 1))
    dy_own = reorder(out_grad, 1)
    half = 2 * shard_rows
    dy_a = gather(dy_own[:, :half])
    dy_b = gather(dy_own[:, half:])
    wg = [reorder(w_gate[e], 0) for e in experts]
    wu = [reorder(w_up[e], 0) for e in experts]
    wd = [reorder(w_down[e], 0) for e in experts]

    meta_b = all_meta.reshape(n_owner, tok_rows, 2 * topk).astype(F32)
    ids_b = meta_b[..., :topk].astype(jnp.int32)
    probs_b = meta_b[..., topk:]
    mine = me_q * local_exp + jnp.arange(local_exp, dtype=jnp.int32)
    hit = ids_b[:, None, :, :] == mine[None, :, None, None]
    picked = jnp.any(hit, axis=3)
    p_tok = jnp.sum(jnp.where(hit, probs_b[:, None], 0.0), axis=3)
    earlier = (
        jnp.arange(tok_rows)[:, None] < jnp.arange(tok_rows)[None, :]
    ).astype(BF16)
    position = mm("bes,st->bet", picked.astype(BF16), earlier).astype(jnp.int32)
    spot = jnp.where(picked, position, capacity)
    slots = n_owner * capacity
    taken, disp, p_slot = [], [], []
    for e in experts:
        fits = spot[:, e, None, :] == jnp.arange(capacity)[None, :, None]
        taken.append(fits)
        disp.append(fits.astype(BF16))
        p_slot.append(
            jnp.sum(jnp.where(fits, p_tok[:, e, None, :], 0.0), axis=2).reshape(slots, 1)
        )

    def dispatch(e, rows_all):
        rows = rows_all.reshape(n_owner, tok_rows, rows_all.shape[1])
        return mm("bct,btd->bcd", disp[e], rows, BF16).reshape(slots, rows_all.shape[1])

    rows_x, act, dact, hid, hid_p = [], [], [], [], []
    for e in experts:
        rows_x.append(dispatch(e, x_all))
        gate = mm("rd,dh->rh", rows_x[e], wg[e])
        upper = mm("rd,dh->rh", rows_x[e], wu[e])
        sig = jax.nn.sigmoid(gate)
        act.append(gate * sig)
        dact.append(upper * sig * (1.0 + gate * (1.0 - sig)))
        hid.append(act[e] * upper)
        hid_p.append((hid[e] * p_slot[e]).astype(BF16))

    def swap(v, bit):
        return lax.ppermute(v, "dp", [(i, i ^ bit) for i in range(n_group)])

    def term(left, right):
        return mm("rd,rh->dh", left, right, BF16)

    bits = [1 + (e % 2) for e in experts]

    def add_far(near_term, far):
        return (near_term.astype(F32) + far.astype(F32)).astype(BF16)

    def total(own_term, own_got, last):
        return own_term.astype(F32) + own_got.astype(F32) + last.astype(F32)

    flat = hold(dy_a, *hid_p)
    dy_a, hid_p = flat[0], list(flat[1:])
    rows_a = [dispatch(e, dy_a) for e in experts]
    down_far = [swap(term(cut(rows_a[e], 0), hid_p[e]), bits[e]) for e in experts]
    down_own = [
        swap(term(cut(rows_a[e], 1), hid_p[e]), 2) if bits[e] == 2 else None for e in experts
    ]
    flat = hold(dy_b, *down_far)
    dy_b, down_far = flat[0], list(flat[1:])
    rows_b = [dispatch(e, dy_b) for e in experts]
    sent = [term(cut(rows_b[e], 0), hid_p[e]) for e in experts if bits[e] == 1]
    flat = hold(*rows_b, *sent)
    rows_b, sent = list(flat[:local_exp]), list(flat[local_exp:])
    for e in experts:
        if bits[e] == 1:
            down_own[e] = swap(sent.pop(0), 1)

    next_pos = [bits[e] for e in experts]
    own_pos = n_group - 1
    down_last, down_term = [], []
    for e in experts:
        left = cut(rows_a[e], 1) if next_pos[e] == 1 else cut(rows_b[e], 0)
        down_last.append(swap(add_far(term(left, hid_p[e]), down_far[e]), 3 - bits[e]))
        down_term.append(term(cut(rows_b[e], 1), hid_p[e]))

    dprob_slot, dgate, dup = [], [], []
    for e in experts:
        u = mm("rd,dh->rh", jnp.concatenate([rows_a[e], rows_b[e]], axis=1), wd[e])
        dprob_slot.append(jnp.sum(u * hid[e].astype(BF16).astype(F32), axis=1))
        dhid = u * p_slot[e]
        dgate.append((dhid * dact[e]).astype(BF16))
        dup.append((dhid * act[e]).astype(BF16))

    rights = [r for e in experts for r in (dgate[e], dup[e])]
    n_far = len(rights)
    early = [down_own[e] for e in experts if bits[e] == 1]
    flat = list(hold(*rights, down_last[0], *early))
    rights, down_last[0], early = flat[:n_far], flat[n_far], flat[n_far + 1 :]
    for e in experts:
        if bits[e] == 1:
            down_own[e] = early.pop(0)
    who = [e for e in experts for _ in range(2)]
    first_pos = [3 - bits[e] for e in experts]
    send_far = [term(cut(rows_x[e], 0), r) for e, r in zip(who, rights)]
    send_own = [term(cut(rows_x[e], first_pos[e]), r) for e, r in zip(who, rights)]
    flat = list(hold(*send_far, *send_own, *rights, *down_last, *down_own))
    send_far, send_own, late = flat[:n_far], flat[n_far : 2 * n_far], flat[2 * n_far : 3 * n_far]
    down_last = flat[3 * n_far : 3 * n_far + local_exp]
    down_own = flat[3 * n_far + local_exp :]
    got_far = [swap(v, bits[e]) for e, v in zip(who, send_far)]
    got_own = [swap(v, bits[e]) for e, v in zip(who, send_own)]

    late = list(late)
    next_term = [term(cut(rows_x[e], next_pos[e]), r) for e, r in zip(who, rights)]
    own_term = [term(cut(rows_x[e], own_pos), r) for e, r in zip(who, rights)]
    flat = list(hold(*late, *next_term, *own_term, *down_term, *got_far[0::2]))
    late, next_term, own_term = flat[:n_far], flat[n_far : 2 * n_far], flat[2 * n_far : 3 * n_far]
    down_term = flat[3 * n_far : 3 * n_far + local_exp]
    got_far[0::2] = flat[3 * n_far + local_exp :]
    part = 0.0
    for e in experts:
        dx = mm("rh,dh->rd", late[2 * e], wg[e]) + mm("rh,dh->rd", late[2 * e + 1], wu[e])
        dx = dx.astype(BF16).reshape(n_owner, capacity, width)
        part = part + mm("bct,bcd->btd", disp[e], dx)
    part = part.astype(BF16).reshape(n_owner * tok_rows, width)
    away = [add_far(t, v) for t, v in zip(next_term, got_far)]
    flat = list(hold(part, *away, *got_own[0::2]))
    part, away = flat[0], flat[1 : 1 + n_far]
    got_own[0::2] = flat[1 + n_far :]
    last = [swap(v, 3 - bits[e]) for e, v in zip(who, away)]
    summed = lax.psum_scatter(part, "expert", scatter_dimension=0, tiled=True)
    grad_tokens = jnp.concatenate(
        [
            lax.dynamic_slice_in_dim(
                summed, (3 - jnp.bitwise_xor(me_p, s)) * shard_rows, shard_rows, 1
            )
            for s in range(n_group)
        ],
        axis=1,
    )

    g_down = [total(down_term[e], down_own[e], down_last[e]) for e in experts]
    g_rest = [total(t, g, v) for t, g, v in zip(own_term, got_own, last)]
    g_gate, g_up = g_rest[0::2], g_rest[1::2]

    q_tok = jnp.stack(
        [
            jnp.sum(
                jnp.where(taken[e], dprob_slot[e].reshape(n_owner, capacity, 1), 0.0), axis=1
            )
            for e in experts
        ],
        axis=1,
    )
    q_got = lax.all_to_all(q_tok.astype(BF16), "expert", split_axis=0, concat_axis=0, tiled=True)
    q_got = q_got.reshape(n_experts, tok_rows).astype(F32)
    sel = expert_ids[:, :, None] == jnp.arange(n_experts, dtype=jnp.int32)[None, None, :]
    grad_probs = jnp.sum(jnp.where(sel, q_got.T[:, None, :], 0.0), axis=2).astype(BF16)

    rates = decay_mask.astype(F32)

    def update(weights, grads, column):
        out = []
        for e in experts:
            own = weights[e][own_pos * shard_rows :].astype(F32)
            out.append(
                own - step_size * grads[e] - shrink_rate * rates[e, column] * own
            )
        return jnp.stack(out).astype(BF16)

    return (
        grad_tokens,
        grad_probs,
        update(wg, g_gate, 0),
        update(wu, g_up, 1),
        update(wd, g_down, 2),
    )


def solution(mesh):
    placed = (
        P(("dp", "expert"), None),
        P(("dp", "expert"), None),
        P(("dp", "expert"), None),
        P(("dp", "expert"), None),
        P("expert", None, None),
        P("expert", None, None),
        P("expert", None, None),
        P("expert", None),
    )
    return jax.shard_map(
        body,
        mesh=mesh,
        in_specs=placed,
        out_specs=(
            P(("dp", "expert"), None),
            P(("dp", "expert"), None),
            P("expert", "dp", None),
            P("expert", "dp", None),
            P("expert", "dp", None),
        ),
        check_vma=False,
    )
```
